32 devices in a mesh: dp: 2 (over core), blk: 16 (over z, y, x).
Axes of the slice: x: 2, y: 2, z: 4, core: 2. Of those that a mesh axis runs over, the one named last changes fastest.
Arguments:
- tokens: bfloat16 [8, 2048, 512], P('dp', 'blk'), may hold values from -6 to 6
- attn_gain: float32 [2, 512], replicated, may hold values from 0.5 to 1.5
- attn_bias: float32 [2, 512], replicated, may hold values from -1.25 to 1.25
- w_qkv: bfloat16 [2, 512, 1536], replicated, may hold values from -0.375 to 0.375
- w_out: bfloat16 [2, 512, 512], replicated, may hold values from -2 to 2
- b_out: float32 [2, 512], replicated, may hold values from -1.25 to 1.25
- mlp_gain: float32 [512], replicated, may hold values from 0.5 to 1.5
- mlp_bias: float32 [512], replicated, may hold values from -1.25 to 1.25
- w_up: bfloat16 [512, 2048], replicated, may hold values from -0.25 to 0.25
- b_up: float32 [2048], replicated, may hold values from -1.25 to 1.25
- w_down: bfloat16 [2048, 512], replicated, may hold values from -0.1875 to 0.1875
- b_down: float32 [512], replicated, may hold values from -1.25 to 1.25
- moe_gain: float32 [512], replicated, may hold values from 0.5 to 1.5
- moe_bias: float32 [512], replicated, may hold values from -1.25 to 1.25
- router: bfloat16 [512, 16], replicated, may hold values from -0.1875 to 0.1875
- expert_up: bfloat16 [16, 512, 2048], P('blk'), may hold values from -0.25 to 0.25
- expert_up_bias: float32 [16, 2048], P('blk'), may hold values from -1.25 to 1.25
- expert_down: bfloat16 [16, 2048, 512], P('blk'), may hold values from -3 to 3
- expert_down_bias: float32 [16, 512], P('blk'), may hold values from -6 to 6
- priority: int32 [32, 512], P(('dp', 'blk')), may hold values from 0 to 511, each once within a row
- routes: int32 [8, 2048, 2], P('dp', 'blk'), may hold values from 0 to 15, all different within a row
- out_grad: bfloat16 [8, 2048, 512], P('dp', 'blk'), may hold values from -6 to 6
Outputs:
- result: bfloat16 [8, 2048, 512], P('dp', 'blk')
- tokens_grad: float32 [8, 2048, 512], P('dp', 'blk')
- attn_gain_grad: float32 [2, 512], replicated
- attn_bias_grad: float32 [2, 512], replicated
- w_qkv_grad: float32 [2, 512, 1536], replicated
- w_out_grad: float32 [2, 512, 512], replicated
- b_out_grad: float32 [2, 512], replicated
- mlp_gain_grad: float32 [512], replicated
- mlp_bias_grad: float32 [512], replicated
- w_up_grad: float32 [512, 2048], replicated
- b_up_grad: float32 [2048], replicated
- w_down_grad: float32 [2048, 512], replicated
- b_down_grad: float32 [512], replicated
- moe_gain_grad: float32 [512], replicated
- moe_bias_grad: float32 [512], replicated
- router_grad: float32 [512, 16], replicated
- expert_up_grad: float32 [16, 512, 2048], P('blk', 'dp')
- expert_up_bias_grad: float32 [16, 2048], P('blk', 'dp')
- expert_down_grad: float32 [16, 2048, 512], P('blk', 'dp')
- expert_down_bias_grad: float32 [16, 512], P('blk', 'dp')
- kept_count: int32 [16], replicated
- dropped_count: int32 [16], replicated
The draws below stay inside these ranges and needn't reach their ends.
Inputs may be any that keep to these rules, and one draw needn't show every extreme that they name: `priority`: each row is a permutation: the ranks of one routing group's tokens, image-major. `routes`: the two experts of a patch differ.
All inputs are finite; a program needn't handle non-finite values.
Results may differ from the reference program's by a relative error of at most 0.019.
Values may be sent and summed in bfloat16 or wider, within the bound.
No kernel may reach another device: no remote copies, remote signals or barrier semaphores. Data moves between devices by JAX's collectives and lax.ppermute only.
A program may use at most 192 MiB of HBM per device.

```python
import jax
import jax.numpy as jnp
from jax import lax

D = 512
HEADS = 8
FF = 2048
IMGS = 4
PATCH = 128
EXPERTS = 16
IMAGES = 8
LENGTH = 2048
CAP = 68
N_DP = 2
N_BLK = 16
DEVICES = 32


def steps_of(own_key, shape, cuts, low, high):
    def one(dim, parts):
        steps = jax.random.uniform(jax.random.fold_in(jax.random.fold_in(own_key, 6), dim), (parts,), jnp.float32, low / len(cuts), high / len(cuts))
        return jnp.repeat(jnp.exp(steps), shape[dim] // parts).reshape((-1,) + (1,) * (len(shape) - dim - 1))

    gain = one(*cuts[0])
    for cut in cuts[1:]:
        gain = gain * one(*cut)
    return gain


def picks_of(stream_key, rows, number_of, top, lift):
    order = jax.random.permutation(jax.random.fold_in(stream_key, 1), number_of)
    boost = order
    for power in range(3):
        boost = boost * boost // number_of
    boost = boost * lift // number_of
    tickets = jax.random.randint(jax.random.fold_in(stream_key, 2), (rows, number_of), 0, 4096) + boost
    fixed_rows = jax.random.permutation(jax.random.fold_in(stream_key, 3), rows)[jnp.arange(number_of) % rows]
    tickets = jnp.where(jnp.arange(rows)[:, None] == fixed_rows[None, :], 1 << 14, tickets)
    merit = tickets * number_of + jnp.arange(number_of)
    return lax.top_k(merit.astype(jnp.int32), top)[1].astype(jnp.int32)


def gaussian(rng, dims, scale, reach, cuts=(), kind=jnp.bfloat16):
    values = jax.random.normal(rng, dims, jnp.float32) * scale
    if len(cuts) > 0:
        values = steps_of(rng, dims, cuts, -0.22, 0.18) * values
    return jnp.clip(values, min=-reach, max=reach).astype(kind)


def setup_inputs(seed: int = 0) -> dict:
    seeds = jax.random.split(jax.random.key(seed), 23)
    return {
        "tokens": gaussian(seeds[0], (IMAGES, LENGTH, D), 1.0, 6.0, ((0, 2), (1, 16))),
        "attn_gain": jnp.clip(1.0 + 0.1 * jax.random.normal(seeds[1], (2, D), jnp.float32), 0.5, 1.5),
        "attn_bias": gaussian(seeds[2], (2, D), 0.2, 1.25, (), jnp.float32),
        "w_qkv": gaussian(seeds[3], (2, D, 3 * D), (D // 2) ** -0.5, 0.375),
        "w_out": gaussian(seeds[4], (2, D, D), (D // 64) ** -0.5, 2.0),
        "b_out": gaussian(seeds[5], (2, D), 0.2, 1.25, (), jnp.float32),
        "mlp_gain": jnp.clip(1.0 + 0.1 * jax.random.normal(seeds[6], (D,), jnp.float32), 0.5, 1.5),
        "mlp_bias": gaussian(seeds[7], (D,), 0.2, 1.25, (), jnp.float32),
        "w_up": gaussian(seeds[8], (D, FF), D ** -0.5, 0.25),
        "b_up": gaussian(seeds[9], (FF,), 0.2, 1.25, (), jnp.float32),
        "w_down": gaussian(seeds[10], (FF, D), (FF // 2) ** -0.5, 0.1875),
        "b_down": gaussian(seeds[11], (D,), 0.2, 1.25, (), jnp.float32),
        "moe_gain": jnp.clip(1.0 + 0.1 * jax.random.normal(seeds[12], (D,), jnp.float32), 0.5, 1.5),
        "moe_bias": gaussian(seeds[13], (D,), 0.2, 1.25, (), jnp.float32),
        "router": gaussian(seeds[14], (D, EXPERTS), (2 * D) ** -0.5, 0.1875),
        "expert_up": gaussian(seeds[15], (EXPERTS, D, FF), D ** -0.5, 0.25, ((0, 16),)),
        "expert_up_bias": gaussian(seeds[16], (EXPERTS, FF), 0.2, 1.25, ((0, 16),), jnp.float32),
        "expert_down": gaussian(seeds[17], (EXPERTS, FF, D), (max(FF // 512, 1)) ** -0.5, 3.0, ((0, 16),)),
        "expert_down_bias": gaussian(seeds[18], (EXPERTS, D), 1.0, 6.0, ((0, 16),), jnp.float32),
        "priority": jax.vmap(lambda own: jax.random.permutation(own, IMGS * PATCH))(jax.random.split(seeds[19], DEVICES)).reshape((DEVICES, IMGS * PATCH)).astype(jnp.int32),
        "routes": picks_of(seeds[20], IMAGES * LENGTH, EXPERTS, 2, 2048).reshape((IMAGES, LENGTH, 2)),
        "out_grad": gaussian(seeds[21], (IMAGES, LENGTH, D), 1.0, 6.0, ((0, 2), (1, 16))),
    }


@jax.custom_vjp
def low(v):
    return lax.optimization_barrier(v.astype(jnp.bfloat16)).astype(jnp.float32)

@jax.custom_vjp
def low_back(v):
    return v

def low_keep(v):
    return (low(v), None)

def low_pass(kept, grad):
    return (grad,)

def back_keep(v):
    return (v, None)

def back_low(kept, grad):
    return (low(grad),)
low.defvjp(low_keep, low_pass)
low_back.defvjp(back_keep, back_low)
highest = lax.Precision.HIGHEST
epsilon = 1e-06

def layer_norm(stream, norm_gain, norm_bias):
    centre = lax.optimization_barrier(jnp.mean(stream, axis=-1, keepdims=True))
    shifted = stream - centre
    spread = lax.optimization_barrier(jnp.mean(shifted * shifted, axis=-1, keepdims=True))
    return shifted * lax.rsqrt(spread + epsilon) * norm_gain + norm_bias

def softmax_rows(logits):
    largest = lax.optimization_barrier(jnp.max(logits, axis=-1, keepdims=True))
    weights = jnp.exp(logits - largest)
    return weights / lax.optimization_barrier(jnp.sum(weights, axis=-1, keepdims=True))

def gelu_exact(values):
    return jax.nn.gelu(values, approximate=False)

def place_slots(ranking, choices, experts, capacity):
    tok_count = ranking.shape[0]
    order = jnp.zeros((tok_count,), jnp.int32).at[ranking].set(jnp.arange(tok_count, dtype=jnp.int32))
    ordered = choices[order]
    labels = jnp.arange(experts, dtype=jnp.int32)
    first = (ordered[:, 0:1] == labels[None, :]).astype(jnp.int32)
    second = (ordered[:, 1:2] == labels[None, :]).astype(jnp.int32)
    first_before = (jnp.cumsum(first, axis=0) - first).astype(jnp.int32)
    second_before = (jnp.cumsum(second, axis=0) - second + lax.optimization_barrier(jnp.sum(first, axis=0, keepdims=True))).astype(jnp.int32)
    first_place = lax.optimization_barrier(jnp.sum(first_before * first, axis=1)).astype(jnp.int32)
    second_place = lax.optimization_barrier(jnp.sum(second_before * second, axis=1)).astype(jnp.int32)
    position = jnp.stack([first_place, second_place], axis=1)[ranking]
    kept = position < capacity
    places = jnp.where(kept, choices * capacity + position, experts * capacity - 1).astype(jnp.int32)
    kept_int = kept.astype(jnp.int32)
    matches = (choices[:, :, None] == labels[None, None, :]).astype(jnp.int32)
    kept_hits = lax.optimization_barrier(jnp.sum(matches * kept_int[:, :, None], axis=(0, 1))).astype(jnp.int32)
    dropped_hits = (lax.optimization_barrier(jnp.sum(matches, axis=(0, 1))) - kept_hits).astype(jnp.int32)
    return (places, kept.astype(jnp.float32), kept_hits, dropped_hits)

def to_groups(array):
    tail = array.shape[2:]
    split = array.reshape((N_DP, IMGS, N_BLK, PATCH) + tail)
    return jnp.swapaxes(split, 1, 2).reshape((N_DP * N_BLK, IMGS * PATCH) + tail)

def from_groups(array):
    tail = array.shape[2:]
    split = array.reshape((N_DP, N_BLK, IMGS, PATCH) + tail)
    return jnp.swapaxes(split, 1, 2).reshape((N_DP * IMGS, N_BLK * PATCH) + tail)

def attend_block(query_block, key_heads, value_heads):
    scores = low_back(jnp.einsum('hqc,hkc->hqk', query_block, key_heads, precision=highest) * 0.125)
    weights = softmax_rows(scores)
    return jnp.einsum('hqk,hkc->hqc', low(weights), value_heads, precision=highest)

def attention_branch(image, norm_gain, norm_bias, qkv_weight, out_weight, out_bias):
    head_size = D // HEADS
    normed = low(layer_norm(image, norm_gain, norm_bias))
    mixed = low(low_back(jnp.dot(normed, qkv_weight, precision=highest)))
    mixed = mixed.reshape(LENGTH, HEADS, 3, head_size).transpose(2, 1, 0, 3)
    row_block = min(512, LENGTH)
    query_blocks = mixed[0].reshape(HEADS, LENGTH // row_block, row_block, head_size).transpose(1, 0, 2, 3)

    def one_block(query_block):
        return attend_block(query_block, mixed[1], mixed[2])
    outputs = lax.map(jax.checkpoint(one_block), query_blocks)
    attended = low(low_back(outputs.transpose(0, 2, 1, 3).reshape(LENGTH, D)))
    return low_back(jnp.dot(attended, out_weight, precision=highest) + out_bias)

def mlp_branch(image, norm_gain, norm_bias, up_weight, up_bias, down_weight, down_bias):
    normed = low(layer_norm(image, norm_gain, norm_bias))
    hidden = low_back(jnp.dot(normed, up_weight, precision=highest) + up_bias)
    activated = low(gelu_exact(hidden))
    return low_back(jnp.dot(activated, down_weight, precision=highest) + down_bias)

def expert_apply(pieces):
    slot_rows, up_weight, up_bias, down_weight, down_bias = pieces
    slot_rows = low_back(slot_rows)
    hidden = low_back(jnp.dot(slot_rows, up_weight, precision=highest) + up_bias)
    activated = low(gelu_exact(hidden))
    return low(low_back(jnp.dot(activated, down_weight, precision=highest) + down_bias))

def mixture(grouped, norm_gain, norm_bias, router, expert_up, expert_up_bias, expert_down, expert_down_bias, choices, places, kept):
    group_count = grouped.shape[0]
    tok_count = grouped.shape[1]
    normed = low(layer_norm(grouped, norm_gain, norm_bias))
    logits = low_back(jnp.einsum('gtd,de->gte', normed, router, precision=highest))
    gates = softmax_rows(logits)
    gate_value = jnp.take_along_axis(gates, choices, axis=-1) * kept
    sent_rows = jnp.broadcast_to(normed[:, :, None, :], (group_count, tok_count, 2, D)) * kept[:, :, :, None]
    sent_rows = sent_rows.reshape(group_count, 2 * tok_count, D)
    flat_places = places.reshape(group_count, 2 * tok_count)

    def fill(row_group, place_group):
        return jnp.zeros((EXPERTS * CAP, D), jnp.float32).at[place_group].add(row_group)
    buffer = jax.vmap(fill)(sent_rows, flat_places)
    expert_rows = buffer.reshape(group_count, EXPERTS, CAP, D).transpose(1, 0, 2, 3).reshape(EXPERTS, group_count * CAP, D)
    results = lax.map(jax.checkpoint(expert_apply), (expert_rows, expert_up, expert_up_bias, expert_down, expert_down_bias))
    table = results.reshape(EXPERTS, group_count, CAP, D).transpose(1, 0, 2, 3).reshape(group_count, EXPERTS * CAP, D)

    def pick(table_group, place_group):
        return table_group[place_group]
    picked = jax.vmap(pick)(table, flat_places).reshape(group_count, tok_count, 2, D)
    return grouped + lax.optimization_barrier(jnp.sum(gate_value[..., None] * picked, axis=2))

def forward(stream, params, choices, places, kept):
    attn_gain, attn_bias, w_qkv, w_out, b_out, mlp_gain, mlp_bias, w_up, b_up, w_down, b_down, moe_gain, moe_bias, router, expert_up, expert_up_bias, expert_down, expert_down_bias = params

    def first_attention(image):
        return attention_branch(image, attn_gain[0], attn_bias[0], w_qkv[0], w_out[0], b_out[0])

    def feed_forward(image):
        return mlp_branch(image, mlp_gain, mlp_bias, w_up, b_up, w_down, b_down)

    def second_attention(image):
        return attention_branch(image, attn_gain[1], attn_bias[1], w_qkv[1], w_out[1], b_out[1])
    stream = stream + lax.map(first_attention, stream)
    stream = stream + lax.map(feed_forward, stream)
    stream = stream + lax.map(second_attention, stream)
    grouped = to_groups(stream)
    mixed = mixture(grouped, moe_gain, moe_bias, router, expert_up, expert_up_bias, expert_down, expert_down_bias, choices, places, kept)
    return from_groups(mixed)

def group_slots(ranking, choices):
    return place_slots(ranking, choices, EXPERTS, CAP)

def reference(tokens, attn_gain, attn_bias, w_qkv, w_out, b_out, mlp_gain, mlp_bias, w_up, b_up, w_down, b_down, moe_gain, moe_bias, router, expert_up, expert_up_bias, expert_down, expert_down_bias, priority, routes, out_grad):
    params = (attn_gain.astype(jnp.float32), attn_bias.astype(jnp.float32), w_qkv.astype(jnp.float32), w_out.astype(jnp.float32), b_out.astype(jnp.float32), mlp_gain.astype(jnp.float32), mlp_bias.astype(jnp.float32), w_up.astype(jnp.float32), b_up.astype(jnp.float32), w_down.astype(jnp.float32), b_down.astype(jnp.float32), moe_gain.astype(jnp.float32), moe_bias.astype(jnp.float32), router.astype(jnp.float32), expert_up.astype(jnp.float32), expert_up_bias.astype(jnp.float32), expert_down.astype(jnp.float32), expert_down_bias.astype(jnp.float32))
    choices = to_groups(routes)
    places, kept, kept_hits, dropped_hits = jax.vmap(group_slots)(priority, choices)
    kept_count = lax.optimization_barrier(jnp.sum(kept_hits, axis=0)).astype(jnp.int32)
    dropped_count = lax.optimization_barrier(jnp.sum(dropped_hits, axis=0)).astype(jnp.int32)

    def whole(stream, weights):
        return forward(stream, weights, choices, places, kept)
    result, pullback = jax.vjp(whole, tokens.astype(jnp.float32), params)
    stream_grad, grads = pullback(out_grad.astype(jnp.float32))
    return (result.astype(jnp.bfloat16), stream_grad, grads[0], grads[1], grads[2], grads[3], grads[4], grads[5], grads[6], grads[7], grads[8], grads[9], grads[10], grads[11], grads[12], grads[13], grads[14], grads[15], grads[16], grads[17], kept_count, dropped_count)
```

```python
import math

import jax
import jax.numpy as jnp
from jax import lax
from jax.experimental import pallas as pl
from jax.experimental.pallas import tpu as pltpu
from jax.sharding import PartitionSpec as P

HEADS = 8

epsilon = 1e-06
log2_e = 1.4426950408889634
MIB = 1024 * 1024


def split3(values):
    high = values.astype(jnp.bfloat16)
    rest = values - high.astype(jnp.float32)
    middle = rest.astype(jnp.bfloat16)
    low = (rest - middle.astype(jnp.float32)).astype(jnp.bfloat16)
    return (high, middle, low)


def abt(left, right):
    return lax.dot_general(
        left, right, (((1,), (1,)), ((), ())), preferred_element_type=jnp.float32
    )


def ab(left, right):
    return jnp.dot(left, right, preferred_element_type=jnp.float32)


def atb(left, right):
    return lax.dot_general(
        left, right, (((0,), (0,)), ((), ())), preferred_element_type=jnp.float32
    )


def normalize(stream):
    centre = jnp.mean(stream, axis=1, keepdims=True)
    shifted = stream - centre
    spread = jnp.mean(shifted * shifted, axis=1, keepdims=True)
    scale = lax.rsqrt(spread + epsilon)
    return (shifted * scale, scale)


def norm_back(stream, norm_gain, normed_grad):
    hat, scale = normalize(stream)
    gain_grad = jnp.sum(normed_grad * hat, axis=0, keepdims=True)
    bias_grad = jnp.sum(normed_grad, axis=0, keepdims=True)
    inner = normed_grad * norm_gain
    along = jnp.mean(inner * hat, axis=1, keepdims=True)
    level = jnp.mean(inner, axis=1, keepdims=True)
    return (scale * (inner - level - hat * along), gain_grad, bias_grad)


def gelu_parts(values):
    size = jnp.abs(values)
    bell = jnp.exp2(values * values * (-0.5 * log2_e))
    t = 1.0 / (1.0 + size * (0.3275911 * math.sqrt(0.5)))
    series = t * (
        0.127414796
        + t * (-0.142248368 + t * (0.7107068705 + t * (-0.7265760135 + t * 0.5307027145)))
    )
    tail = series * bell
    cdf = jnp.where(values < 0, tail, 1.0 - tail)
    return (values * cdf, cdf + values * bell * (1.0 / math.sqrt(2.0 * math.pi)))


def call(kernel, name, operands, outs, flops, grid=(1,), specs=None, out_specs=None, scratch=(), limit=60):
    whole = lambda shape: pl.BlockSpec(shape, lambda *steps: (0,) * len(shape))
    specs = dict(specs or {})
    out_specs = out_specs or {}
    for number, operand in enumerate(operands):
        if operand.dtype == jnp.int32 and operand.shape == (1,):
            specs[number] = pl.BlockSpec(memory_space=pltpu.SMEM)
    return pl.pallas_call(
        kernel,
        grid=grid,
        in_specs=[specs.get(i, whole(array.shape)) for i, array in enumerate(operands)],
        out_specs=[out_specs.get(i, whole(out.shape)) for i, out in enumerate(outs)],
        out_shape=outs,
        scratch_shapes=list(scratch),
        compiler_params=pltpu.CompilerParams(vmem_limit_bytes=limit * MIB),
        cost_estimate=pl.CostEstimate(
            flops=flops,
            bytes_accessed=sum(a.size * a.dtype.itemsize for a in operands)
            + sum(o.size * o.dtype.itemsize for o in outs),
            transcendentals=0,
        ),
        name=name,
    )(*operands)


def layer_spec(array, layer):
    return pl.BlockSpec((None,) + array.shape[1:], lambda *steps: (layer, 0, 0))


def bf16(*shape):
    return jax.ShapeDtypeStruct(shape, jnp.bfloat16)


def f32(*shape):
    return jax.ShapeDtypeStruct(shape, jnp.float32)


def ahead(place, shift, count):
    return lax.rem(place + shift, count)


def block_at(number, size):
    return pl.ds(pl.multiple_of(number * size, size), size)


def attention_block(length):
    return min(length, 2**21 // length)


def attention(mixed, head_size, local_heads, order):
    length = mixed.shape[0]
    block = attention_block(length)
    scale = head_size**-0.5

    def kernel(mixed_ref, out_ref, plain_ref, query_ref, keys, values):
        step = pl.program_id(0)

        @pl.when(step == 0)
        def _():
            for head in range(local_heads):
                base = head * 3 * head_size
                key = mixed_ref[:, base + head_size : base + 2 * head_size]
                value = mixed_ref[:, base + 2 * head_size : base + 3 * head_size]
                keys[head] = jnp.concatenate([key, key], axis=1)
                values[head] = jnp.concatenate(
                    [value, jnp.ones((length, head_size), jnp.bfloat16)], axis=1
                )

        rows = pl.ds(pl.multiple_of(step * block, block), block)
        scores = []
        for head in range(local_heads):
            base = head * 3 * head_size
            query = mixed_ref[rows, base : base + head_size].astype(jnp.float32) * (scale * log2_e)
            high = query.astype(jnp.bfloat16)
            low = (query - high.astype(jnp.float32)).astype(jnp.bfloat16)
            pair = jnp.concatenate([high, low], axis=1)
            query_ref[:, head * 4 * head_size : head * 4 * head_size + 2 * head_size] = pair
            scores.append(abt(pair, keys[head]))
        outs = []
        for head in range(local_heads):
            largest = jnp.max(scores[head], axis=1, keepdims=True)
            weights = jnp.exp2(scores[head] - largest).astype(jnp.bfloat16)
            total = ab(weights, values[head])
            sums = total[:, head_size : head_size + 1]
            outs.append(total[:, :head_size] / sums)
            log_sum = largest + jnp.log2(sums)
            lane = lax.broadcasted_iota(jnp.int32, (block, 2 * head_size), 1)
            extra = jnp.zeros((block, 2 * head_size), jnp.float32)
            for place, digit in enumerate(split3(log_sum)):
                extra = jnp.where(lane == place, digit.astype(jnp.float32), extra)
            query_ref[:, head * 4 * head_size + 2 * head_size : (head + 1) * 4 * head_size] = (
                extra.astype(jnp.bfloat16)
            )
        both = jnp.concatenate(outs, axis=1)
        plain_ref[...] = both
        both = both.astype(jnp.bfloat16)
        if order is None:
            out_ref[rows, :] = both
        else:
            images, per = order
            size = length // (images * per)
            count = block // size
            for piece in range(count):
                number = step * count + piece
                place = lax.rem(number, images) * per + lax.div(number, images)
                target = pl.ds(pl.multiple_of(place * size, size), size)
                out_ref[target, :] = both[piece * size : (piece + 1) * size]

    return call(
        kernel,
        "attention",
        [mixed],
        [
            bf16(length, local_heads * head_size),
            f32(length, local_heads * head_size),
            bf16(length, local_heads * 4 * head_size),
        ],
        local_heads * length * length * 16 * head_size,
        grid=(length // block,),
        out_specs={
            1: pl.BlockSpec((block, local_heads * head_size), lambda step: (step, 0)),
            2: pl.BlockSpec((block, local_heads * 4 * head_size), lambda step: (step, 0)),
        },
        scratch=[
            pltpu.VMEM((local_heads, length, 2 * head_size), jnp.bfloat16),
            pltpu.VMEM((local_heads, length, 2 * head_size), jnp.bfloat16),
        ],
    )


def attention_back(mixed, queries, outs, grads, head_size, local_heads, order, flops):
    length = mixed.shape[0]
    block = attention_block(length)
    chunk = length // 4
    scale = head_size**-0.5

    def kernel(
        mixed_hbm, query_hbm, out_hbm, grad_hbm, mixed_grad_ref, grads, query_grads, weights,
        score_grads, mixed_ref, query_ref, out_ref, grad_ref, semaphores,
    ):
        step = pl.program_id(0)

        @pl.when(step == 0)
        def _():
            copies = [
                pltpu.make_async_copy(source, target, semaphores.at[place])
                for place, (source, target) in enumerate(
                    [
                        (grad_hbm, grad_ref), (out_hbm, out_ref), (mixed_hbm, mixed_ref),
                        (query_hbm, query_ref),
                    ]
                )
            ]
            for copy in copies:
                copy.start()
            copies[0].wait()
            copies[1].wait()
            query_grads[...] = jnp.zeros_like(query_grads)
            pieces = [(0, 0, length)]
            if order is not None:
                images, per = order
                size = length // (images * per)
                pieces = [
                    ((row * per + column) * size, (column * images + row) * size, size)
                    for row in range(images)
                    for column in range(per)
                ]
            for source, target, size in pieces:
                for head in range(local_heads):
                    columns = slice(head * head_size, (head + 1) * head_size)
                    grad = grad_ref[source : source + size, columns]
                    out = out_ref[target : target + size, columns]
                    dots = jnp.sum(grad.astype(jnp.float32) * out, axis=1, keepdims=True)
                    lane = lax.broadcasted_iota(jnp.int32, (size, head_size), 1)
                    extra = jnp.zeros((size, head_size), jnp.float32)
                    for place, digit in enumerate(split3(dots)):
                        extra = jnp.where(lane == place, digit.astype(jnp.float32), extra)
                    grads[head, target : target + size, :] = jnp.concatenate(
                        [grad, extra.astype(jnp.bfloat16)], axis=1
                    )
            copies[2].wait()
            copies[3].wait()

        rows = pl.ds(pl.multiple_of(step * block, block), block)
        for head in range(local_heads):
            base = head * 3 * head_size
            key = mixed_ref[rows, base + head_size : base + 2 * head_size]
            value = mixed_ref[rows, base + 2 * head_size : base + 3 * head_size]
            lane = lax.broadcasted_iota(jnp.int32, (block, 2 * head_size), 1)
            minus = jnp.where(lane < 3, -1.0, 0.0).astype(jnp.bfloat16)
            keys = jnp.concatenate([key, key, minus], axis=1)
            values = jnp.concatenate([value, minus[:, :head_size]], axis=1)
            for piece in range(length // chunk):
                span = slice(piece * chunk, (piece + 1) * chunk)
                scores = abt(keys, query_ref[span, head * 4 * head_size : (head + 1) * 4 * head_size])
                weight = jnp.exp2(scores)
                weights[head, :, span] = weight.astype(jnp.bfloat16)
                score_grads[head, :, span] = (weight * abt(values, grads[head, span, :])).astype(
                    jnp.bfloat16
                )
        for head in range(local_heads):
            base = head * 3 * head_size
            key = mixed_ref[rows, base + head_size : base + 2 * head_size]
            turned = key.astype(jnp.float32).T.astype(jnp.bfloat16)
            value_grad = ab(weights[head], grads[head])
            key_grad = ab(score_grads[head], mixed_ref[:, base : base + head_size])
            query_grads[head] += ab(turned, score_grads[head])
            mixed_grad_ref[rows, base + head_size : base + 3 * head_size] = jnp.concatenate(
                [key_grad * scale, value_grad[:, :head_size]], axis=1
            ).astype(jnp.bfloat16)

        @pl.when(step == pl.num_programs(0) - 1)
        def _():
            for head in range(local_heads):
                base = head * 3 * head_size
                mixed_grad_ref[:, base : base + head_size] = (query_grads[head] * scale).T.astype(
                    jnp.bfloat16
                )

    return call(
        kernel,
        "attention_back",
        [mixed, queries, outs, grads],
        [bf16(*mixed.shape)],
        flops,
        grid=(length // block,),
        specs={number: pl.BlockSpec(memory_space=pl.ANY) for number in range(4)},
        scratch=[
            pltpu.VMEM((local_heads, length, 2 * head_size), jnp.bfloat16),
            pltpu.VMEM((local_heads, head_size, length), jnp.float32),
            pltpu.VMEM((local_heads, block, length), jnp.bfloat16),
            pltpu.VMEM((local_heads, block, length), jnp.bfloat16),
        ]
        + [pltpu.VMEM(array.shape, array.dtype) for array in (mixed, queries, outs, grads)]
        + [pltpu.SemaphoreType.DMA((4,))],
    )[0]


def project(stream, gains, biases, w_qkv, layer, per):
    tokens, width = stream.shape
    columns = w_qkv.shape[2] // per

    def kernel(stream_ref, gain_ref, bias_ref, weight_ref, mixed_ref, normed_ref):
        hat, unused = normalize(stream_ref[...].astype(jnp.float32))
        normed = (hat * gain_ref[layer : layer + 1] + bias_ref[layer : layer + 1]).astype(
            jnp.bfloat16
        )
        normed_ref[...] = normed
        for part in range(per):
            mixed_ref[part] = ab(
                normed, weight_ref[:, part * columns : (part + 1) * columns]
            ).astype(jnp.bfloat16)

    return call(
        kernel,
        "project",
        [stream, gains, biases, w_qkv],
        [bf16(per, tokens, columns), bf16(tokens, width)],
        2 * tokens * width * w_qkv.shape[2],
        specs={3: layer_spec(w_qkv, layer)},
    )


def middle_forward(
    me, images, parts, start, w_out, b_out, mlp_gain, mlp_bias, w_up, b_up, w_down, b_down, gains,
    biases, w_qkv,
):
    per, tokens, out_columns = parts.shape
    patches = tokens // images
    width = start.shape[1]
    hidden_width = w_up.shape[1]
    columns = w_qkv.shape[2] // per
    chunk = hidden_width // 2

    def kernel(
        me_ref, parts_ref, start_ref, w_out_ref, b_out_ref, mlp_gain_ref, mlp_bias_ref, w_up_ref,
        b_up_ref, w_down_ref, b_down_ref, gain_ref, bias_ref, weight_ref,
        first_ref, mlp_normed_ref, act_ref, slope_ref, second_ref, normed_ref, mixed_ref,
        *piece_refs,
    ):
        attended = jnp.concatenate([parts_ref[part] for part in range(per)], axis=1)
        first = start_ref[...].astype(jnp.float32) + ab(attended, w_out_ref[...]) + b_out_ref[0:1]
        first_ref[...] = first
        hat, unused = normalize(first)
        mlp_normed = (hat * mlp_gain_ref[...] + mlp_bias_ref[...]).astype(jnp.bfloat16)
        mlp_normed_ref[...] = mlp_normed
        second = first + b_down_ref[...]
        for piece in range(hidden_width // chunk):
            span = slice(piece * chunk, (piece + 1) * chunk)
            act, slope = gelu_parts(ab(mlp_normed, w_up_ref[:, span]) + b_up_ref[:, span])
            act = act.astype(jnp.bfloat16)
            act_ref[:, span] = act
            slope_ref[:, span] = slope.astype(jnp.bfloat16)
            second += ab(act, w_down_ref[span, :])
        second_ref[...] = second
        for shift, piece_ref in enumerate(piece_refs):
            rows = block_at(ahead(me_ref[0], shift, images), patches)
            piece_ref[...] = second_ref[rows, :].astype(jnp.bfloat16)
        hat, unused = normalize(second)
        normed = (hat * gain_ref[1:2] + bias_ref[1:2]).astype(jnp.bfloat16)
        normed_ref[...] = normed
        for part in range(per):
            mixed_ref[part] = ab(
                normed, weight_ref[:, part * columns : (part + 1) * columns]
            ).astype(jnp.bfloat16)

    return call(
        kernel,
        "middle_forward",
        [
            me, parts, start, w_out, b_out, mlp_gain, mlp_bias, w_up, b_up, w_down, b_down, gains,
            biases, w_qkv,
        ],
        [
            f32(tokens, width),
            bf16(tokens, width),
            bf16(tokens, hidden_width),
            bf16(tokens, hidden_width),
            f32(tokens, width),
            bf16(tokens, width),
            bf16(per, tokens, columns),
        ]
        + [bf16(patches, width)] * images,
        2 * tokens * width * (width + 2 * hidden_width + w_qkv.shape[2]),
        specs={3: layer_spec(w_out, 0), 13: layer_spec(w_qkv, 1)},
    )


def middle_back(
    me, grad_parts, pieces, second, first, slope, gains, mlp_gain, w_qkv, w_down, w_up, w_out
):
    per, tokens, columns = grad_parts.shape
    width = second.shape[1]
    hidden_width = w_up.shape[1]
    out_columns = width // per
    chunk = hidden_width // 2
    images = len(pieces)
    patches = tokens // images

    def kernel(
        me_ref, parts_ref, second_ref, first_ref, slope_ref, gain_ref, mlp_gain_ref, weight_ref,
        w_down_ref, w_up_ref, w_out_ref, *refs,
    ):
        piece_refs = refs[:images]
        (
            sent_ref, first_grad_ref, branch_ref, down_grad_ref, hidden_grad_ref, sums_ref,
            up_sum_ref, upper_ref,
        ) = refs[images:]
        for shift, piece_ref in enumerate(piece_refs):
            rows = block_at(ahead(me_ref[0], images - shift, images), patches)
            upper_ref[rows, :] = piece_ref[...]
        normed_grad = jnp.zeros((tokens, width), jnp.float32)
        for part in range(per):
            normed_grad += abt(
                parts_ref[part], weight_ref[:, part * columns : (part + 1) * columns]
            )
        back, gain_grad, bias_grad = norm_back(second_ref[...], gain_ref[1:2], normed_grad)
        second_grad = upper_ref[...].astype(jnp.float32) + back
        down_grad = second_grad.astype(jnp.bfloat16)
        down_grad_ref[...] = down_grad
        normed_grad = jnp.zeros((tokens, width), jnp.float32)
        for piece in range(hidden_width // chunk):
            span = slice(piece * chunk, (piece + 1) * chunk)
            hidden_grad = (
                abt(down_grad, w_down_ref[span, :]) * slope_ref[:, span].astype(jnp.float32)
            ).astype(jnp.bfloat16)
            hidden_grad_ref[:, span] = hidden_grad
            up_sum_ref[:, span] = jnp.sum(
                hidden_grad.astype(jnp.float32), axis=0, keepdims=True
            )
            normed_grad += abt(hidden_grad, w_up_ref[:, span])
        back, mlp_gain_grad, mlp_bias_grad = norm_back(
            first_ref[...], mlp_gain_ref[...], normed_grad
        )
        first_grad = second_grad + back
        first_grad_ref[...] = first_grad
        branch = first_grad.astype(jnp.bfloat16)
        branch_ref[...] = branch
        for part in range(per):
            sent_ref[part] = abt(
                branch, w_out_ref[part * out_columns : (part + 1) * out_columns, :]
            ).astype(jnp.bfloat16)
        row = lambda array: jnp.sum(array.astype(jnp.float32), axis=0, keepdims=True)
        sums = [gain_grad, bias_grad, mlp_gain_grad, mlp_bias_grad, row(down_grad), row(branch)]
        sums_ref[...] = jnp.concatenate(sums + [jnp.zeros((2, width), jnp.float32)], axis=0)

    return call(
        kernel,
        "middle_back",
        [
            me, grad_parts, second, first, slope, gains, mlp_gain, w_qkv, w_down, w_up, w_out,
        ]
        + list(pieces),
        [
            bf16(per, tokens, out_columns),
            f32(tokens, width),
            bf16(tokens, width),
            bf16(tokens, width),
            bf16(tokens, hidden_width),
            f32(8, width),
            f32(1, hidden_width),
        ],
        2 * tokens * width * (width + 2 * hidden_width + w_qkv.shape[2]),
        specs={7: layer_spec(w_qkv, 1), 10: layer_spec(w_out, 0)},
        scratch=[pltpu.VMEM((tokens, width), jnp.bfloat16)],
    )


def final_back(me, images, grad_parts, first_grad, start, gains, w_qkv):
    per, tokens, columns = grad_parts.shape
    width = start.shape[1]
    patches = tokens // images

    def kernel(
        me_ref, parts_ref, first_grad_ref, start_ref, gain_ref, weight_ref, sums_ref, *refs
    ):
        piece_refs, grad_ref = refs[:images], refs[images]
        normed_grad = jnp.zeros((tokens, width), jnp.float32)
        for part in range(per):
            normed_grad += abt(
                parts_ref[part], weight_ref[:, part * columns : (part + 1) * columns]
            )
        back, gain_grad, bias_grad = norm_back(
            start_ref[...].astype(jnp.float32), gain_ref[0:1], normed_grad
        )
        grad_ref[...] = (first_grad_ref[...] + back).astype(jnp.bfloat16)
        for shift, piece_ref in enumerate(piece_refs):
            piece_ref[...] = grad_ref[block_at(ahead(me_ref[0], shift, images), patches), :]
        sums_ref[...] = jnp.concatenate(
            [gain_grad, bias_grad, jnp.zeros((6, width), jnp.float32)], axis=0
        )

    return call(
        kernel,
        "final_back",
        [me, grad_parts, first_grad, start, gains, w_qkv],
        [f32(8, width)] + [bf16(patches, width)] * images,
        2 * tokens * width * w_qkv.shape[2],
        specs={5: layer_spec(w_qkv, 0)},
        scratch=[pltpu.VMEM((tokens, width), jnp.bfloat16)],
    )


def gather_pieces(me, pieces):
    images = len(pieces)
    patches, width = pieces[0].shape

    def kernel(me_ref, *refs):
        for shift in range(images):
            place = ahead(me_ref[0], images - shift, images)
            refs[images][place] = refs[shift][...].astype(jnp.float32)

    return call(
        kernel, "gather_pieces", [me] + list(pieces), [f32(images, patches, width)], 1
    )[0]


def side_by_side(parts_ref):
    return jnp.concatenate([parts_ref[part] for part in range(parts_ref.shape[0])], axis=1)


def weight_grads(
    normed1, grad_parts1, mlp_normed, hidden_grad, act, down_grad, attended1, branch1, parts0,
    branch0,
):
    tokens, width = normed1.shape
    hidden_width = act.shape[1]
    columns = grad_parts1.shape[0] * grad_parts1.shape[2]

    def kernel(
        normed_ref, grad_ref, mlp_normed_ref, hidden_grad_ref, act_ref, down_grad_ref,
        attended_ref, branch1_ref, parts_ref, branch0_ref, qkv_ref, up_ref, down_ref, out_ref,
    ):
        turned = mlp_normed_ref[...].T
        for block in range(hidden_width // width):
            span = slice(block * width, (block + 1) * width)
            up_ref[:, span] = ab(turned, hidden_grad_ref[:, span]).astype(jnp.bfloat16)
            down_ref[span, :] = ab(act_ref[:, span].T, down_grad_ref[...]).astype(jnp.bfloat16)
        turned = normed_ref[...].T
        for part in range(grad_ref.shape[0]):
            span = slice(part * grad_ref.shape[2], (part + 1) * grad_ref.shape[2])
            qkv_ref[:, span] = ab(turned, grad_ref[part]).astype(jnp.bfloat16)
        out_ref[0] = ab(side_by_side(parts_ref).T, branch0_ref[...]).astype(jnp.bfloat16)
        out_ref[1] = ab(attended_ref[...].T, branch1_ref[...]).astype(jnp.bfloat16)

    return call(
        kernel,
        "weight_grads",
        [
            normed1, grad_parts1, mlp_normed, hidden_grad, act, down_grad, attended1, branch1,
            parts0, branch0,
        ],
        [
            bf16(width, columns),
            bf16(width, hidden_width),
            bf16(hidden_width, width),
            bf16(2, width, width),
        ],
        2 * tokens * width * (columns + 2 * hidden_width + 2 * width),
    )


def last_grads(normed0, grad_parts0, out_grads, small):
    tokens, width = normed0.shape
    rows = small.shape[0]

    def kernel(normed_ref, grad_ref, out_grad_ref, small_ref, rows_ref):
        turned = normed_ref[...].T
        mixed_grad = side_by_side(grad_ref)
        for block in range(3):
            span = slice(block * width, (block + 1) * width)
            rows_ref[span, :] = ab(turned, mixed_grad[:, span]).astype(jnp.bfloat16)
        for block in range(2):
            rows_ref[(3 + block) * width : (4 + block) * width, :] = out_grad_ref[block]
        rows_ref[5 * width :, :] = small_ref[...]

    return call(
        kernel,
        "last_grads",
        [normed0, grad_parts0, out_grads, small],
        [bf16(5 * width + rows, width)],
        2 * tokens * width * width * 3,
    )[0]


def finish(up, down, qkv1, rows):
    width, hidden_width = up.shape
    steps = 4
    band = width // steps

    def kernel(up_ref, down_ref, qkv1_ref, *refs):
        blocks = refs[:5]
        up_out, down_out, qkv_out, proj_out = refs[5:]
        up_out[...] = up_ref[...].astype(jnp.float32)
        down_out[...] = down_ref[...].astype(jnp.float32)
        for block in range(3):
            qkv_out[0, :, block * width : (block + 1) * width] = blocks[block][...].astype(
                jnp.float32
            )
        qkv_out[1] = qkv1_ref[...].astype(jnp.float32)
        proj_out[0] = blocks[3][...].astype(jnp.float32)
        proj_out[1] = blocks[4][...].astype(jnp.float32)

    row_band = lambda size, columns: pl.BlockSpec((size, columns), lambda step: (step, 0))
    block_band = lambda block: pl.BlockSpec((band, width), lambda step: (block * steps + step, 0))
    layers = lambda columns: pl.BlockSpec((2, band, columns), lambda step: (0, step, 0))
    specs = {
        0: row_band(band, hidden_width),
        1: row_band(hidden_width // steps, width),
        2: row_band(band, 3 * width),
    }
    for block in range(5):
        specs[3 + block] = block_band(block)
    return call(
        kernel,
        "finish",
        [up, down, qkv1] + [rows] * 5,
        [
            f32(width, hidden_width),
            f32(hidden_width, width),
            f32(2, width, 3 * width),
            f32(2, width, width),
        ],
        1,
        grid=(steps,),
        specs=specs,
        out_specs={
            0: specs[0],
            1: specs[1],
            2: layers(3 * width),
            3: layers(width),
        },
    )


def slot_rows_of(capacity):
    return (capacity + 3 + 7) // 8 * 8


def place_slots(priority, choices, capacity, experts, top):
    tokens, width = top.shape
    half = width // 2
    span = slot_rows_of(capacity)

    def kernel(row_ref, column_ref, choice_ref, top_ref, target_ref, count_ref, *slot_refs):
        earlier = (column_ref[...] < row_ref[...]).astype(jnp.bfloat16)
        expert = lax.broadcasted_iota(jnp.int32, (experts, tokens), 0)
        picks = [(choice_ref[k : k + 1, :] == expert).astype(jnp.float32) for k in (0, 1)]
        before = [ab(pick.astype(jnp.bfloat16), earlier) for pick in picks]
        before[1] += jnp.sum(picks[0], axis=1, keepdims=True)
        targets = []
        hits = jnp.zeros((experts, 1), jnp.float32)
        for k in (0, 1):
            position = jnp.sum(before[k] * picks[k], axis=0, keepdims=True).astype(jnp.int32)
            kept = position < capacity
            targets.append(jnp.where(kept, choice_ref[k : k + 1, :] * span + position, -1))
            hits += jnp.sum(picks[k] * kept.astype(jnp.float32), axis=1, keepdims=True)
        misses = jnp.sum(picks[0] + picks[1], axis=1, keepdims=True) - hits
        target_ref[...] = jnp.concatenate(targets, axis=0)
        count_ref[...] = jnp.concatenate([hits, misses], axis=1)
        slot = lax.broadcasted_iota(jnp.int32, (experts * span, tokens), 0)
        taken = ((slot == targets[0]) | (slot == targets[1])).astype(jnp.bfloat16)
        for part, slots_ref in enumerate(slot_refs):
            slots_ref[...] = ab(taken, top_ref[:, part * half : (part + 1) * half]).astype(
                jnp.bfloat16
            )

    return call(
        kernel,
        "place_slots",
        [priority.reshape(1, tokens), priority.reshape(tokens, 1), choices.T, top],
        [
            jax.ShapeDtypeStruct((2, tokens), jnp.int32),
            f32(experts, 2),
            bf16(experts * span, half),
            bf16(experts * span, half),
        ],
        2 * tokens * experts * span * width,
    )


def upper_forward(
    me, parts, pieces, w_out, b_out, gain, bias, router_rows, targets, capacity
):
    blocks, patches, out_columns = parts.shape
    images = len(pieces)
    per = blocks // images
    tokens, width = images * patches, pieces[0].shape[1]
    experts = router_rows.shape[0]
    span = slot_rows_of(capacity)

    def kernel(
        me_ref, parts_ref, w_out_ref, b_out_ref, gain_ref, bias_ref, router_ref, target_ref, *refs
    ):
        piece_refs = refs[:images]
        upper_ref, normed_ref, gate_ref, slots_ref, attended_ref = refs[images:]
        for shift, piece_ref in enumerate(piece_refs):
            rows = block_at(ahead(me_ref[0], images - shift, images), patches)
            upper_ref[rows, :] = piece_ref[...].astype(jnp.float32)
        for image in range(images):
            attended_ref[image * patches : (image + 1) * patches, :] = jnp.concatenate(
                [parts_ref[image * per + part] for part in range(per)], axis=1
            )
        upper = upper_ref[...] + ab(attended_ref[...], w_out_ref[...]) + b_out_ref[1:2]
        upper_ref[...] = upper
        hat, unused = normalize(upper)
        normed = (hat * gain_ref[...] + bias_ref[...]).astype(jnp.bfloat16)
        normed_ref[...] = normed
        logits = abt(router_ref[...], normed)
        weights = jnp.exp(logits - jnp.max(logits, axis=0, keepdims=True))
        gates = weights / jnp.sum(weights, axis=0, keepdims=True)
        gate_ref[...] = gates
        digits = [digit.astype(jnp.float32) for digit in split3(gates)]
        row = lax.broadcasted_iota(jnp.int32, (span, width), 0)
        for expert in range(experts):
            slot = lax.broadcasted_iota(jnp.int32, (span, tokens), 0) + expert * span
            taken = (slot == target_ref[0:1, :]) | (slot == target_ref[1:2, :])
            taken = taken.astype(jnp.bfloat16)
            slots = ab(taken, normed)
            digit = jnp.concatenate(
                [digits[place][expert : expert + 1] for place in range(3)]
                + [jnp.zeros((5, tokens), jnp.float32)],
                axis=0,
            ).astype(jnp.bfloat16)
            scalars = abt(digit, taken)
            scalars = jnp.concatenate(
                [scalars, jnp.zeros((8, width - span), jnp.float32)], axis=1
            )
            for place in range(3):
                slots = jnp.where(row == capacity + place, scalars[place : place + 1], slots)
            slots_ref[expert] = slots.astype(jnp.bfloat16)

    return call(
        kernel,
        "upper_forward",
        [me, parts, w_out, b_out, gain, bias, router_rows, targets] + list(pieces),
        [
            f32(tokens, width),
            bf16(tokens, width),
            f32(experts, tokens),
            bf16(experts, span, width),
            bf16(tokens, width),
        ],
        2 * tokens * width * (width + experts * span),
        specs={2: layer_spec(w_out, 1)},
    )


def expert_core(rows, tops, up, up_bias, down, down_bias, capacity):
    groups, span, width = rows.shape
    total = groups * span
    hidden_width = up.shape[2]
    steps = 2
    chunk = hidden_width // steps

    def kernel(
        rows_ref, left_ref, right_ref, up_ref, up_bias_ref, down_ref, down_bias_ref,
        act_ref, hidden_grad_ref, out_grad_ref, rows_grad_ref, up_sum_ref, down_sum_ref,
        gate, gate_grad, rows_grad, top_ref,
    ):
        step = pl.program_id(0)

        @pl.when(step == 0)
        def _():
            lane = lax.broadcasted_iota(jnp.int32, (span, width), 1)
            row = lax.broadcasted_iota(jnp.int32, (span, width), 0)
            for group in range(groups):
                some = slice(group * span, (group + 1) * span)
                values = rows_ref[some, :].astype(jnp.float32)
                scalars = (
                    values[capacity : capacity + 1]
                    + values[capacity + 1 : capacity + 2]
                    + values[capacity + 2 : capacity + 3]
                )
                column = jnp.sum(jnp.where(lane == row, scalars, 0.0), axis=1, keepdims=True)
                gate[some, :] = jnp.where(row[:, :1] < capacity, column, 0.0)
            top_ref[:, : width // 2] = left_ref[...]
            top_ref[:, width // 2 :] = right_ref[...]
            top_rows = top_ref[...].astype(jnp.float32)
            out_grad = (gate[...] * top_rows).astype(jnp.bfloat16)
            out_grad_ref[...] = out_grad
            down_sum_ref[...] = jnp.sum(out_grad.astype(jnp.float32), axis=0, keepdims=True)
            gate_grad[...] = jnp.sum(top_rows * down_bias_ref[...], axis=1, keepdims=True)
            rows_grad[...] = jnp.zeros_like(rows_grad)

        up_piece = up_ref[...]
        act, slope = gelu_parts(ab(rows_ref[...], up_piece) + up_bias_ref[...])
        act = act.astype(jnp.bfloat16)
        act_ref[...] = act
        plain = abt(top_ref[...], down_ref[...])
        gate_grad[...] += jnp.sum(act.astype(jnp.float32) * plain, axis=1, keepdims=True)
        hidden_grad = (gate[...] * plain * slope).astype(jnp.bfloat16)
        hidden_grad_ref[...] = hidden_grad
        up_sum_ref[...] = jnp.sum(hidden_grad.astype(jnp.float32), axis=0, keepdims=True)
        rows_grad[...] += abt(hidden_grad, up_piece)

        @pl.when(step == steps - 1)
        def _():
            lane = lax.broadcasted_iota(jnp.int32, (span, width), 1)
            row = lax.broadcasted_iota(jnp.int32, (span, width), 0)
            for group in range(groups):
                some = slice(group * span, (group + 1) * span)
                scalars = jnp.sum(
                    jnp.where((lane == row) & (row < capacity), gate_grad[some, :], 0.0),
                    axis=0,
                    keepdims=True,
                )
                values = rows_grad[some, :]
                for place, digit in enumerate(split3(scalars)):
                    values = jnp.where(
                        row == capacity + place, digit.astype(jnp.float32), values
                    )
                rows_grad[some, :] = values
            rows_grad_ref[...] = rows_grad[...].astype(jnp.bfloat16)

    column_block = lambda rows_of: pl.BlockSpec((rows_of, chunk), lambda step: (0, step))
    return call(
        kernel,
        "expert_core",
        [rows.reshape(total, width)]
        + [top.reshape(total, width // 2) for top in tops]
        + [up, up_bias, down, down_bias],
        [
            bf16(total, hidden_width),
            bf16(total, hidden_width),
            bf16(total, width),
            bf16(total, width),
            f32(1, hidden_width),
            f32(1, width),
        ],
        6 * total * width * hidden_width,
        grid=(steps,),
        specs={
            3: pl.BlockSpec((None, width, chunk), lambda step: (0, 0, step)),
            4: column_block(1),
            5: pl.BlockSpec((None, chunk, width), lambda step: (0, step, 0)),
        },
        out_specs={0: column_block(total), 1: column_block(total), 4: column_block(1)},
        scratch=[
            pltpu.VMEM((total, 1), jnp.float32),
            pltpu.VMEM((total, 1), jnp.float32),
            pltpu.VMEM((total, width), jnp.float32),
            pltpu.VMEM((total, width), jnp.bfloat16),
        ],
    )


def upper_back(
    me, slot_grads, targets, target_columns, gates, normed, upper, top, gain, router_rows, w_out,
    capacity, images, per,
):
    experts, span, width = slot_grads.shape
    tokens = normed.shape[0]
    patches = tokens // images
    out_columns = width // per

    def kernel(
        me_ref, slot_ref, target_ref, column_ref, gate_ref, normed_ref, upper_ref, top_ref,
        gain_ref, router_ref, w_out_ref,
        attended_grad_ref, branch_ref, router_grad_ref, sums_ref, *piece_refs,
    ):
        slot = lax.broadcasted_iota(jnp.int32, (tokens, experts * span), 1)
        taken = (slot == column_ref[:, 0:1]) | (slot == column_ref[:, 1:2])
        normed_grad = ab(taken.astype(jnp.bfloat16), slot_ref[...])
        gates_grad = []
        for expert in range(experts):
            scalars = slot_ref[expert * span : (expert + 1) * span, :].astype(jnp.float32)
            scalars = scalars[capacity : capacity + 3, :span]
            scalars = jnp.concatenate(
                [scalars, jnp.zeros((5, span), jnp.float32)], axis=0
            ).astype(jnp.bfloat16)
            place = lax.broadcasted_iota(jnp.int32, (span, tokens), 0) + expert * span
            here = (place == target_ref[0:1, :]) | (place == target_ref[1:2, :])
            spread = ab(scalars, here.astype(jnp.bfloat16))
            gates_grad.append(jnp.sum(spread, axis=0, keepdims=True))
        gates_grad = jnp.concatenate(gates_grad, axis=0)
        gates = gate_ref[...]
        logit_grad = gates * (gates_grad - jnp.sum(gates_grad * gates, axis=0, keepdims=True))
        logit_grad = logit_grad.astype(jnp.bfloat16)
        router_grad_ref[...] = ab(logit_grad, normed_ref[...])
        normed_grad += atb(logit_grad, router_ref[...])
        back, gain_grad, bias_grad = norm_back(upper_ref[...], gain_ref[...], normed_grad)
        branch = (back + top_ref[...].astype(jnp.float32)).astype(jnp.bfloat16)
        branch_ref[...] = branch
        for shift, piece_ref in enumerate(piece_refs):
            piece_ref[...] = branch_ref[block_at(ahead(me_ref[0], shift, images), patches), :]
        attended_grad = abt(branch, w_out_ref[...]).astype(jnp.bfloat16)
        for image in range(images):
            for part in range(per):
                attended_grad_ref[image * per + part] = attended_grad[
                    image * patches : (image + 1) * patches,
                    part * out_columns : (part + 1) * out_columns,
                ]
        shift = jnp.sum(branch.astype(jnp.float32), axis=0, keepdims=True)
        sums_ref[...] = jnp.concatenate(
            [gain_grad, bias_grad, shift, jnp.zeros((5, width), jnp.float32)], axis=0
        )

    return call(
        kernel,
        "upper_back",
        [
            me, slot_grads.reshape(experts * span, width), targets, target_columns, gates, normed,
            upper, top, gain, router_rows, w_out,
        ],
        [
            bf16(images * per, patches, out_columns),
            bf16(tokens, width),
            f32(experts, width),
            f32(8, width),
        ]
        + [bf16(patches, width)] * images,
        2 * tokens * width * (width + experts * span),
        specs={10: layer_spec(w_out, 1)},
    )


def combine(table, target_columns, choices, gates, upper):
    experts, span, width = table.shape
    tokens = upper.shape[0]

    def kernel(table_ref, column_ref, choice_ref, gate_ref, upper_ref, out_ref):
        gates = gate_ref[...].T
        total = upper_ref[...]
        slot = lax.broadcasted_iota(jnp.int32, (tokens, experts * span), 1)
        expert = lax.broadcasted_iota(jnp.int32, (tokens, experts), 1)
        for k in (0, 1):
            taken = (slot == column_ref[:, k : k + 1]).astype(jnp.bfloat16)
            gate = jnp.sum(
                jnp.where(expert == choice_ref[:, k : k + 1], gates, 0.0), axis=1, keepdims=True
            )
            total += gate * ab(taken, table_ref[...])
        out_ref[...] = total.astype(jnp.bfloat16)

    return call(
        kernel,
        "combine",
        [table.reshape(experts * span, width), target_columns, choices, gates, upper],
        [bf16(tokens, width)],
        4 * tokens * width * experts * span,
    )[0]


def plane_groups(blocks, images):
    per = blocks // images
    return [[row * per + column for column in range(per)] for row in range(images)]


def line_groups(blocks, images):
    per = blocks // images
    return [[row * per + column for row in range(images)] for column in range(per)]


def swap(array, groups=None):
    return lax.all_to_all(
        array, "blk", split_axis=0, concat_axis=0, tiled=True, axis_index_groups=groups
    )


def tie(*arrays):
    return lax.optimization_barrier(arrays)


def sum_all(array, plane, line):
    width = array.shape[1]
    stages = (("dp", None), ("blk", plane), ("blk", line))

    def count(axis, groups):
        return lax.axis_size(axis) if groups is None else len(groups[0])

    for axis, groups in stages:
        parts = array.reshape(count(axis, groups), -1, width)
        parts = lax.all_to_all(parts, axis, 0, 0, tiled=True, axis_index_groups=groups)
        array = jnp.sum(parts.astype(jnp.float32), axis=0).astype(jnp.bfloat16)
    for axis, groups in reversed(stages):
        parts = jnp.broadcast_to(array[None], (count(axis, groups),) + array.shape)
        parts = lax.all_to_all(parts, axis, 0, 0, tiled=True, axis_index_groups=groups)
        array = parts.reshape(-1, width)
    return array


def send_ahead(pieces, groups):
    out = [pieces[0]]
    for shift in range(1, len(pieces)):
        pairs = [
            (member, group[(place + shift) % len(group)])
            for group in groups
            for place, member in enumerate(group)
        ]
        out.append(lax.ppermute(pieces[shift], "blk", pairs))
    return out


def count_bits(counts, width):
    bits = (counts.reshape(-1)[:, None].astype(jnp.int32) >> jnp.arange(10, dtype=jnp.int32)) & 1
    flat = bits.reshape(-1).astype(jnp.float32)
    return jnp.pad(flat, (0, -flat.size % width)).reshape(-1, width)


def count_sums(rows, number):
    bits = rows.reshape(-1)[: number * 10].reshape(number, 10).astype(jnp.float32)
    return jnp.sum(bits * (2.0 ** jnp.arange(10)), axis=1).astype(jnp.int32)


def per_device(
    tokens,
    attn_gain,
    attn_bias,
    w_qkv,
    w_out,
    b_out,
    mlp_gain,
    mlp_bias,
    w_up,
    b_up,
    w_down,
    b_down,
    moe_gain,
    moe_bias,
    router,
    expert_up,
    expert_up_bias,
    expert_down,
    expert_down_bias,
    priority,
    routes,
    out_grad,
):
    images, patches, width = tokens.shape
    tok_count = images * patches
    blocks = lax.axis_size("blk")
    per = blocks // images
    local_heads = HEADS // per
    head_size = width // HEADS
    plane = plane_groups(blocks, images)
    line = line_groups(blocks, images)
    experts = router.shape[1]
    capacity = (21 * tok_count + 10 * experts - 1) // (10 * experts)
    span = slot_rows_of(capacity)
    row = lambda vector: vector.reshape(1, -1)
    me = (lax.axis_index("blk") // per).astype(jnp.int32).reshape(1)
    router_rows = router.T
    choices = routes.reshape(tok_count, 2)
    top = out_grad.reshape(tok_count, width)

    start = swap(tokens, line).reshape(tok_count, width)

    targets, counts, left_slots, right_slots = place_slots(
        priority, choices, capacity, experts, top
    )
    target_columns = targets.T
    start, left_slots, target_columns = tie(start, left_slots, target_columns)

    mixed0, normed0 = project(start, attn_gain, attn_bias, w_qkv, 0, per)
    arrived0 = swap(mixed0, plane).reshape(blocks * patches, -1)
    arrived0, left_slots = tie(arrived0, left_slots)
    left_top = swap(left_slots.reshape(experts, span, width // 2))
    out0, plain0, queries0 = attention(arrived0, head_size, local_heads, None)
    out0, left_top = tie(out0, left_top)
    parts0 = swap(out0.reshape(per, tok_count, -1), plane)

    parts0, right_slots = tie(parts0, right_slots)
    right_top = swap(right_slots.reshape(experts, span, width // 2))
    first, mlp_normed, act, slope, second, normed1, mixed1, *pieces = middle_forward(
        me, images, parts0, start, w_out, b_out, row(mlp_gain), row(mlp_bias), w_up, row(b_up),
        w_down, row(b_down), attn_gain, attn_bias, w_qkv,
    )
    mixed1, right_top = tie(mixed1, right_top)
    arrived1 = swap(mixed1, plane).reshape(blocks * patches, -1)
    pieces = send_ahead(pieces, line)
    out1, plain1, queries1 = attention(arrived1, head_size, local_heads, (images, per))
    out1, *pieces = tie(out1, *pieces)
    parts1 = swap(out1.reshape(blocks, patches, -1))

    upper, moe_normed, gates, slots, attended1 = upper_forward(
        me, parts1, pieces, w_out, b_out, row(moe_gain), row(moe_bias), router_rows, targets,
        capacity,
    )
    expert_rows = swap(slots)
    expert_act, hidden_grad, out_rows_grad, rows_grad, up_bias_sum, down_bias_sum = expert_core(
        expert_rows, (left_top, right_top), expert_up, expert_up_bias, expert_down, expert_down_bias, capacity
    )
    slot_grads = swap(rows_grad.reshape(blocks, span, width))
    expert_result = (
        jnp.dot(expert_act, expert_down[0], preferred_element_type=jnp.float32) + expert_down_bias
    ).astype(jnp.bfloat16)
    down_sum = jnp.einsum(
        "rf,rd->fd", expert_act, out_rows_grad, preferred_element_type=jnp.float32
    ).astype(jnp.bfloat16)
    up_sum = jnp.einsum(
        "rd,rf->df",
        expert_rows.reshape(blocks * span, width),
        hidden_grad,
        preferred_element_type=jnp.float32,
    ).astype(jnp.bfloat16)
    slot_grads, expert_result, down_sum, up_sum = tie(slot_grads, expert_result, down_sum, up_sum)
    sent1, upper_branch, router_sum, upper_sums, *pieces = upper_back(
        me, slot_grads, targets, target_columns, gates, moe_normed, upper, top, row(moe_gain),
        router_rows, w_out, capacity, images, per,
    )
    expert_sums = [
        lax.psum_scatter(part.astype(jnp.bfloat16), "dp", scatter_dimension=1, tiled=True).astype(
            jnp.float32
        )
        for part in (up_sum[None], up_bias_sum, down_sum[None], down_bias_sum)
    ]

    grads1 = swap(sent1).reshape(blocks * patches, -1)
    pieces = send_ahead(pieces, line)
    grads1, expert_result = tie(grads1, expert_result)
    table = swap(expert_result.reshape(blocks, span, width))
    mixed_grad1 = attention_back(
        arrived1, queries1, plain1, grads1, head_size, local_heads, (images, per),
        40 * head_size * local_heads * (blocks * patches) ** 2,
    )
    mixed_grad1, table, *pieces = tie(mixed_grad1, table, *pieces)
    grad_parts1 = swap(mixed_grad1.reshape(per, tok_count, -1), plane)
    grad_parts1, *expert_sums = tie(grad_parts1, *expert_sums)

    sent0, first_grad, first_branch, down_grad, mlp_hidden_grad, middle_sums, up_bias_row = (
        middle_back(
            me, grad_parts1, pieces, second, first, slope, attn_gain,
            row(mlp_gain), w_qkv, w_down, w_up, w_out,
        )
    )
    grads0 = swap(sent0, plane).reshape(blocks * patches, -1)
    second_qkv, up_weight_sum, down_weight_sum, out_grads = weight_grads(
        normed1, grad_parts1, mlp_normed, mlp_hidden_grad, act, down_grad, attended1,
        upper_branch, parts0, first_branch,
    )
    grads0, second_qkv = tie(grads0, second_qkv)
    second_qkv, up_weight_sum, down_weight_sum = lax.psum(
        (second_qkv, up_weight_sum, down_weight_sum), ("dp", "blk")
    )

    def last_part(step, carry):
        step, grads, projections, rows_of_slots = tie(step, grads0, out_grads, table)
        mixed_grad0 = attention_back(
            arrived0, queries0, plain0, grads, head_size, local_heads, None, 1
        )
        grad_parts0 = swap(mixed_grad0.reshape(per, tok_count, -1), plane)
        final = combine(rows_of_slots, target_columns, choices, gates, upper)
        first_sums, *pieces = final_back(
            me, images, grad_parts0, first_grad, start, attn_gain, w_qkv
        )
        pieces = send_ahead(pieces, line)
        small = jnp.concatenate(
            [
                upper_sums[0:3],
                middle_sums[0:6],
                first_sums[0:2],
                up_bias_row.reshape(-1, width),
                router_sum,
                count_bits(counts, width),
            ]
        )
        small = jnp.pad(small, ((0, small_rows - small.shape[0]), (0, 0))).astype(jnp.bfloat16)
        rows = last_grads(normed0, grad_parts0, projections, small)
        rows = sum_all(rows, plane, line)
        return (rows, gather_pieces(me, pieces), final)

    devices = 8 * blocks * lax.axis_size("dp")
    small_rows = 11 + w_up.shape[1] // width + experts + -(-20 * experts // width)
    small_rows += -small_rows % devices
    trips = jnp.minimum(priority[0, 0], 0) + 1
    rows, start_group, final = lax.fori_loop(
        0,
        trips,
        last_part,
        (
            jnp.zeros((5 * width + small_rows, width), jnp.bfloat16),
            second.reshape(images, patches, width),
            upper_branch,
        ),
    )
    up_weight_sum, down_weight_sum, qkv_sum, proj_sum = finish(
        up_weight_sum, down_weight_sum, second_qkv, rows
    )
    hidden_rows = w_up.shape[1] // width
    wide = rows[5 * width :].astype(jnp.float32)
    router_at = 11 + hidden_rows
    count_rows = -(-20 * experts // width)
    bits = wide[router_at + experts : router_at + experts + count_rows]
    number = count_sums(bits, 2 * experts).reshape(experts, 2)
    return (
        final.reshape(images, patches, width),
        start_group,
        jnp.stack([wide[9], wide[3]]),
        jnp.stack([wide[10], wide[4]]),
        qkv_sum,
        proj_sum,
        jnp.stack([wide[8], wide[2]]),
        wide[5],
        wide[6],
        up_weight_sum,
        wide[11:router_at].reshape(-1),
        down_weight_sum,
        wide[7],
        wide[0],
        wide[1],
        wide[router_at : router_at + experts].T,
        expert_sums[0],
        expert_sums[1],
        expert_sums[2],
        expert_sums[3],
        number[:, 0],
        number[:, 1],
    )


def solution(mesh):
    return jax.shard_map(
        per_device,
        mesh=mesh,
        in_specs=(
            P("dp", "blk", None),
            P(),
            P(),
            P(),
            P(),
            P(),
            P(),
            P(),
            P(),
            P(),
            P(),
            P(),
            P(),
            P(),
            P(),
            P("blk", None, None),
            P("blk", None),
            P("blk", None, None),
            P("blk", None),
            P(("dp", "blk"), None),
            P("dp", "blk", None),
            P("dp", "blk", None),
        ),
        out_specs=(
            P("dp", "blk", None),
            P("dp", "blk", None),
            P(),
            P(),
            P(),
            P(),
            P(),
            P(),
            P(),
            P(),
            P(),
            P(),
            P(),
            P(),
            P(),
            P(),
            P("blk", "dp", None),
            P("blk", "dp"),
            P("blk", "dp", None),
            P("blk", "dp"),
            P(),
            P(),
        ),
        check_vma=False,
    )
```
